256 devices in a mesh: rep: 32 (over y, z_lo, core), fsdp: 8 (over x, z_hi).
Axes of the slice: x: 4, y: 4, z: 8 (z_hi: 2, z_lo: 4; z = z_hi * 4 + z_lo), core: 2. Of those that a mesh axis runs over, the one named last changes fastest.
Arguments:
- tokens: bfloat16 [32, 2, 3072, 4096], P('rep', None, 'fsdp'), may hold values from -6 to 6
- token_ids: int32 [32, 2, 3072], P('rep', None, 'fsdp'), may hold values from 0 to 128004, as said below
- out_grad: bfloat16 [32, 2, 3072, 512], P('rep', None, 'fsdp'), may hold values from -6 to 6
- local_weight: bfloat16 [32, 4096, 512], P('rep', 'fsdp'), may hold values from -6 to 6
- adam_first: float32 [32, 4096, 512], P('rep', 'fsdp'), may hold values from -4 to 4
- adam_second: float32 [32, 4096, 512], P('rep', 'fsdp'), may hold values from 0.05 to 2
- anchor: float32 [4096, 512], P('fsdp'), may hold values from -6 to 6
- outer_momentum: float32 [4096, 512], P('fsdp'), may hold values from -4 to 4
- fragment: int32 [1], replicated, may hold values from 0 to 1
Outputs:
- new_local: bfloat16 [32, 4096, 512], P('rep', 'fsdp')
- new_first: float32 [32, 4096, 512], P('rep', 'fsdp')
- new_second: float32 [32, 4096, 512], P('rep', 'fsdp')
- new_anchor: float32 [4096, 512], P('fsdp')
- new_momentum: float32 [4096, 512], P('fsdp')
The draws below stay inside these ranges and needn't reach their ends.
Inputs may be any that keep to these rules, and one draw needn't show every extreme that they name: `token_ids`: each device's 384 tokens of one inner step form one sequence: regular ids below 128000, then the padding id 128004 to its end; at least a quarter of them are regular and at least the last one is padding.
All inputs are finite; a program needn't handle non-finite values.
Results may differ from the reference program's by a relative error of at most 0.015.
Values may be sent and summed in bfloat16 or wider, within the bound.
No kernel may reach another device: no remote copies, remote signals or barrier semaphores. Data moves between devices by JAX's collectives and lax.ppermute only.
A program may use at most 128 MiB of HBM per device.

```python
import math
import jax
import jax.numpy as jnp
from jax import lax

D = 4096
KVW = 512
FRAGS = 2
STEPS = 2
TOK_DEV = 384
REPS = 32
TOKENS_REP = 3072
N_REP = 32


def draw_token_ids(key, part):
    key = jax.random.fold_in(key, 7)
    key_length, key_regular = jax.random.split(key)
    blocks = TOKENS_REP // TOK_DEV
    lengths = jax.random.randint(key_length, (REPS, STEPS, blocks, 1), TOK_DEV // 4, TOK_DEV)
    regular = jax.random.randint(key_regular, (REPS, STEPS, blocks, TOK_DEV), 0, 128000)
    position = lax.broadcasted_iota(jnp.int32, (REPS, STEPS, blocks, TOK_DEV), 3)
    return jnp.where(position < lengths, regular, 128004).reshape(REPS, STEPS, TOKENS_REP).astype(jnp.int32)


def spiked(result, own_key, source, target, shards_of, factor):
    owner, partner = [(jnp.arange(result.shape[axis_at]) // (result.shape[axis_at] // shards_of)).reshape([-1 if axis == axis_at else 1 for axis in range(result.ndim)]) for axis_at in (source, target)]
    chosen = jax.random.permutation(own_key, shards_of)[partner]
    strong = (owner == chosen) | (owner == (partner + shards_of // 2) % shards_of)
    return jnp.where(strong, factor * result, result)


def steps_of(own_key, dims, cuts, low, largest):
    gain, own = 1.0, jax.random.fold_in(own_key, 6)
    for axis_at, parts in cuts:
        draws = jnp.exp(jax.random.uniform(jax.random.fold_in(own, axis_at), (parts,), jnp.float32, low / len(cuts), largest / len(cuts)))
        gain = gain * jnp.repeat(draws, dims[axis_at] // parts).reshape([-1 if axis == axis_at else 1 for axis in range(len(dims))])
    return gain


def centred(own_key, shape, spread, limit, shards=(), dtype=jnp.bfloat16):
    array = spread * jax.random.normal(own_key, shape, jnp.float32)
    if shards:
        array = array * steps_of(own_key, shape, shards, -0.22, 0.18)
    return jnp.clip(array, -limit, limit).astype(dtype)


def noise_with(key, extent, width, bound, shards, heavy, kind=jnp.bfloat16):
    result = width * jax.random.normal(key, extent, jnp.float32)
    if shards:
        result = result * steps_of(key, extent, shards, -0.22, 0.18)
    return jnp.clip(spiked(result, jax.random.fold_in(key, 3), *heavy), -bound, bound).astype(kind)


def setup_inputs(seed: int = 0) -> dict:
    streams_of = jax.random.split(jax.random.key(seed), 10)
    tokens = noise_with(streams_of[0], (REPS, STEPS, TOKENS_REP, D), 1.0, 6.0, ((0, 32), (2, 8)), (2, 3, 8, 2.0))
    token_ids = draw_token_ids(jax.random.fold_in(streams_of[9], 71), 0)
    out_grad = centred(streams_of[2], (REPS, STEPS, TOKENS_REP, KVW), 1.0, 6.0, ((0, 32), (2, 8)))
    local_weight = centred(streams_of[3], (REPS, D, KVW), 1.0, 6.0, ((0, 32), (1, 8)))
    adam_first = centred(streams_of[4], (REPS, D, KVW), 0.5, 4.0, ((0, 32), (1, 8)), jnp.float32)
    adam_second = jnp.clip(jnp.exp(math.log(2.0) - 3.6888794 * jax.random.uniform(streams_of[5], (REPS, D, KVW), jnp.float32) ** steps_of(streams_of[5], (REPS, D, KVW), ((0, 32), (1, 8)), -0.2, 0.2)), 0.05, 2.0)
    anchor = centred(streams_of[6], (D, KVW), 1.0, 6.0, ((0, 8),), jnp.float32)
    outer_momentum = centred(streams_of[7], (D, KVW), 0.5, 4.0, ((0, 8),), jnp.float32)
    fragment = jax.random.randint(streams_of[8], (1,), 0, FRAGS).astype(jnp.int32)
    return {"tokens": tokens, "token_ids": token_ids, "out_grad": out_grad, "local_weight": local_weight, "adam_first": adam_first, "adam_second": adam_second, "anchor": anchor, "outer_momentum": outer_momentum, "fragment": fragment}


beta_first = 0.5
beta_second = 0.95
inner_rate = 0.25
decay_rate = 0.1
adam_eps = 1e-08
outer_rate = 0.7
outer_mu = 0.9
mix_keep = 0.5
pad_token = 128004

def inner_train(operands):
    tokens, token_ids, out_grad, weight, first_moment, second_moment = operands
    proj_scale = 1.0 / math.sqrt(D)
    for inner_step in range(STEPS):
        inputs = tokens[inner_step].astype(jnp.float32)
        scores = proj_scale * jnp.dot(inputs, weight.astype(jnp.float32), precision=lax.Precision.HIGHEST)
        logistic = jax.nn.sigmoid(scores)
        silu_slope = logistic * (1.0 + scores * (1.0 - logistic))
        keep_mask = (token_ids[inner_step] != pad_token).astype(jnp.float32)
        back_signal = (keep_mask[:, None] * out_grad[inner_step].astype(jnp.float32) * silu_slope).astype(jnp.bfloat16)
        gradient = proj_scale * jnp.dot(inputs.T, back_signal.astype(jnp.float32), precision=lax.Precision.HIGHEST)
        first_moment = beta_first * first_moment + (1.0 - beta_first) * gradient
        second_moment = beta_second * second_moment + (1.0 - beta_second) * gradient * gradient
        master = weight.astype(jnp.float32)
        master = master - inner_rate * (first_moment / (jnp.sqrt(second_moment) + adam_eps) + decay_rate * master)
        weight = master.astype(jnp.bfloat16)
    return (weight, first_moment, second_moment)

def reference(tokens, token_ids, out_grad, local_weight, adam_first, adam_second, anchor, outer_momentum, fragment):
    piece_width = KVW // FRAGS
    column = (fragment[0] * piece_width).astype(jnp.int32)
    start_piece = lax.dynamic_slice_in_dim(local_weight, column, piece_width, 2).astype(jnp.float32)
    average = lax.optimization_barrier(jnp.sum(start_piece, axis=0)) / N_REP
    anchor_piece = lax.dynamic_slice_in_dim(anchor, column, piece_width, 1)
    moment_piece = lax.dynamic_slice_in_dim(outer_momentum, column, piece_width, 1)
    pseudo = anchor_piece - average
    moment_new = outer_mu * moment_piece + pseudo
    anchor_new = anchor_piece - outer_rate * (pseudo + outer_mu * moment_new)
    trained, first_moment, second_moment = lax.map(inner_train, (tokens, token_ids, out_grad, local_weight, adam_first, adam_second))
    trained_piece = lax.dynamic_slice_in_dim(trained, column, piece_width, 2)
    mixed_piece = (mix_keep * trained_piece.astype(jnp.float32) + (1.0 - mix_keep) * anchor_new[None]).astype(jnp.bfloat16)
    trained = lax.dynamic_update_slice_in_dim(trained, mixed_piece, column, 2)
    new_anchor = lax.dynamic_update_slice_in_dim(anchor, anchor_new, column, 1)
    new_momentum = lax.dynamic_update_slice_in_dim(outer_momentum, moment_new, column, 1)
    return (trained, first_moment, second_moment, new_anchor, new_momentum)
```

```python
import functools
import math

import jax
import jax.numpy as jnp
from jax import lax
from jax.experimental import pallas as pl
from jax.experimental.pallas import tpu as pltpu
from jax.sharding import PartitionSpec as P

FRAGS = 2
CHUNKS = 2

beta_first = 0.5
beta_second = 0.95
inner_rate = 0.25
decay_rate = 0.1
adam_eps = 1e-08
outer_rate = 0.7
outer_mu = 0.9
mix_keep = 0.5
pad_token = 128004
XS = 4
VMEM = 12 * 1024 * 1024


def z_swap(array):
    return lax.ppermute(array, "fsdp", [(i, i ^ 1) for i in range(2 * XS)])


def x_shift(array, offset):
    pairs = [
        (x * 2 + z, ((x + offset) % XS) * 2 + z) for x in range(XS) for z in range(2)
    ]
    return lax.ppermute(array, "fsdp", pairs)


def rep_swap(array, bit):
    return lax.ppermute(array, "rep", [(i, i ^ bit) for i in range(32)])


def after(value, *earlier):
    return lax.optimization_barrier((value, *earlier))[0]


def params():
    return pltpu.CompilerParams(vmem_limit_bytes=VMEM)


def cost():
    return pl.CostEstimate(flops=1000, bytes_accessed=1000, transcendentals=0)


def copy_body(x_at, *refs):
    for source, target in zip(refs[:XS], refs[XS:], strict=True):
        target[...] = source[0, 0]


def arrange(x_at, tokens, step):
    count, width = tokens.shape[2:]
    cut = width // XS
    tile = count // 2

    def taken(offset):
        return lambda i, x: (0, step, i, lax.rem(x[0] + offset, XS))

    return pl.pallas_call(
        copy_body,
        grid_spec=pltpu.PrefetchScalarGridSpec(
            num_scalar_prefetch=1,
            grid=(count // tile,),
            in_specs=[pl.BlockSpec((1, 1, tile, cut), taken(o)) for o in range(XS)],
            out_specs=[pl.BlockSpec((tile, cut), lambda i, x: (i, 0))] * XS,
        ),
        out_shape=[jax.ShapeDtypeStruct((count, cut), tokens.dtype)] * XS,
        compiler_params=params(),
        cost_estimate=cost(),
    )(x_at, *[tokens] * XS)


def halves_of(block, z_at):
    rows = block.shape[1] // 2
    mine = block[:, pl.ds(pl.multiple_of(z_at * rows, rows), rows)]
    theirs = block[:, pl.ds(pl.multiple_of((1 - z_at) * rows, rows), rows)]
    return mine, theirs


def forward_body(z_at, *refs):
    blocks, (weight, other), parts = refs[:XS], refs[XS : XS + 2], refs[XS + 2 :]
    for block, part in zip(blocks, parts, strict=True):
        mine, theirs = halves_of(block, z_at[0])
        total = jnp.dot(mine, weight[...], preferred_element_type=jnp.float32)
        total += jnp.dot(theirs, other[...], preferred_element_type=jnp.float32)
        part[...] = total.astype(part.dtype)


def forward(z_at, blocks, weight, other, column, chunk):
    count, cut = blocks[0].shape
    rows = cut // 2
    tile = count // 2
    weights = pl.BlockSpec((rows, chunk), lambda i, z: (0, column))
    return pl.pallas_call(
        forward_body,
        grid_spec=pltpu.PrefetchScalarGridSpec(
            num_scalar_prefetch=1,
            grid=(count // tile,),
            in_specs=[pl.BlockSpec((tile, cut), lambda i, z: (i, 0))] * XS + [weights] * 2,
            out_specs=[pl.BlockSpec((tile, chunk), lambda i, z: (i, 0))] * XS,
        ),
        out_shape=[
            jax.ShapeDtypeStruct((count, chunk), jnp.bfloat16 if o else jnp.float32)
            for o in range(XS)
        ],
        compiler_params=params(),
        cost_estimate=cost(),
    )(z_at, *blocks, weight, other)


def slope_body(scale, *refs):
    parts, grads, back = refs[:XS], refs[XS], refs[XS + 1]
    scores = parts[0][...]
    for part in parts[1:]:
        scores += part[...].astype(jnp.float32)
    scores = scale * scores
    logistic = jax.nn.sigmoid(scores)
    slope = logistic * (1.0 + scores * (1.0 - logistic))
    back[...] = (grads[...].astype(jnp.float32) * slope).astype(back.dtype)


def slope(scale, parts, grads, column):
    count, chunk = parts[0].shape
    tile = count // 2
    own = pl.BlockSpec((tile, chunk), lambda i: (i, 0))
    return pl.pallas_call(
        functools.partial(slope_body, scale),
        grid=(count // tile,),
        in_specs=[own] * XS + [pl.BlockSpec((tile, chunk), lambda i: (i, column))],
        out_specs=own,
        out_shape=jax.ShapeDtypeStruct((count, chunk), jnp.bfloat16),
        compiler_params=params(),
        cost_estimate=cost(),
    )(*parts, grads)


def backward_body(scale, z_at, *refs):
    blocks, backs = refs[:XS], refs[XS : 2 * XS]
    mine, theirs, mine_sum, theirs_sum = refs[2 * XS :]
    at = pl.program_id(0)

    @pl.when(at == 0)
    def _():
        mine_sum[...] = jnp.zeros_like(mine_sum)
        theirs_sum[...] = jnp.zeros_like(theirs_sum)

    for total, half in ((theirs_sum, 1), (mine_sum, 0)):
        more = 0.0
        for block, back in zip(blocks, backs, strict=True):
            more += lax.dot_general(
                halves_of(block, z_at[0])[half],
                back[...],
                (((0,), (0,)), ((), ())),
                preferred_element_type=jnp.float32,
            )
        total[...] += more

    @pl.when(at == pl.num_programs(0) - 1)
    def _():
        mine[...] = scale * mine_sum[...]
        theirs[...] = (scale * theirs_sum[...]).astype(theirs.dtype)


def backward(scale, z_at, blocks, backs):
    count, cut = blocks[0].shape
    chunk = backs[0].shape[1]
    rows = cut // 2
    tile = count // 2
    out = pl.BlockSpec((rows, chunk), lambda i, z: (0, 0))
    return pl.pallas_call(
        functools.partial(backward_body, scale),
        grid_spec=pltpu.PrefetchScalarGridSpec(
            num_scalar_prefetch=1,
            grid=(count // tile,),
            in_specs=[pl.BlockSpec((tile, cut), lambda i, z: (i, 0))] * XS
            + [pl.BlockSpec((tile, chunk), lambda i, z: (i, 0))] * XS,
            out_specs=[out, out],
            scratch_shapes=[pltpu.VMEM((rows, chunk), jnp.float32)] * 2,
        ),
        out_shape=[
            jax.ShapeDtypeStruct((rows, chunk), jnp.float32),
            jax.ShapeDtypeStruct((rows, chunk), jnp.bfloat16),
        ],
        compiler_params=params(),
        cost_estimate=cost(),
    )(z_at, *blocks, *backs)


def adam_values(mine, received, first, second, weight):
    grad = mine[...] + received[...].astype(jnp.float32)
    first = beta_first * first[...] + (1.0 - beta_first) * grad
    second = beta_second * second[...] + (1.0 - beta_second) * grad * grad
    master = weight[...].astype(jnp.float32)
    master = master - inner_rate * (
        first / (jnp.sqrt(second) + adam_eps) + decay_rate * master
    )
    return first, second, master.astype(jnp.bfloat16)


def adam_body(mine, received, first, second, weight, first_out, second_out, weight_out):
    first_out[...], second_out[...], weight_out[...] = adam_values(
        mine, received, first, second, weight
    )


def adam(mine, received, first, second, weight, column):
    rows, chunk = mine.shape
    height = rows // 2
    own = pl.BlockSpec((height, chunk), lambda i: (i, 0))
    whole = pl.BlockSpec((height, chunk), lambda i: (i, column))
    return pl.pallas_call(
        adam_body,
        grid=(rows // height,),
        in_specs=[own, own, whole, whole, whole],
        out_specs=[own, own, own],
        out_shape=[
            jax.ShapeDtypeStruct((rows, chunk), jnp.float32),
            jax.ShapeDtypeStruct((rows, chunk), jnp.float32),
            jax.ShapeDtypeStruct((rows, chunk), jnp.bfloat16),
        ],
        compiler_params=params(),
        cost_estimate=cost(),
    )(mine, received, first, second, weight)


def finish_body(
    column, fragment, mine, received, first, second, weight, anchor, *rest
):
    first_out, second_out, weight_out = rest[-3:]
    first_out[...], second_out[...], trained = adam_values(
        mine, received, first, second, weight
    )
    chunk = trained.shape[1]
    lanes = lax.broadcasted_iota(jnp.int32, trained.shape, 1) + column * chunk
    rostered = lanes // (CHUNKS * chunk // FRAGS) == fragment[0]
    mixed = mix_keep * trained.astype(jnp.float32) + (1.0 - mix_keep) * anchor[...]
    weight_out[...] = jnp.where(rostered, mixed.astype(jnp.bfloat16), trained)


def finish(fragment, mine, received, first, second, weight, anchor, earlier, column):
    rows, chunk = mine.shape
    height = rows // 2
    own = pl.BlockSpec((height, chunk), lambda i, f: (i, 0))
    whole = pl.BlockSpec((height, chunk), lambda i, f: (i, column))
    shape = (rows, chunk * CHUNKS)
    return pl.pallas_call(
        functools.partial(finish_body, column),
        grid_spec=pltpu.PrefetchScalarGridSpec(
            num_scalar_prefetch=1,
            grid=(rows // height,),
            in_specs=[own] * 5 + [whole] + [pl.BlockSpec(memory_space=pl.ANY)] * len(earlier),
            out_specs=[whole] * 3,
        ),
        out_shape=[
            jax.ShapeDtypeStruct(shape, jnp.float32),
            jax.ShapeDtypeStruct(shape, jnp.float32),
            jax.ShapeDtypeStruct(shape, jnp.bfloat16),
        ],
        input_output_aliases={7 + i: i for i in range(len(earlier))},
        compiler_params=params(),
        cost_estimate=cost(),
    )(fragment, mine, received, first, second, weight, anchor, *earlier)


def local(
    tokens,
    token_ids,
    out_grad,
    local_weight,
    adam_first,
    adam_second,
    anchor,
    outer_momentum,
    fragment,
):
    steps, token_count, width = tokens.shape[1:]
    proj_scale = 1.0 / math.sqrt(width)
    columns = local_weight.shape[2]
    piece_width = columns // FRAGS
    chunk = columns // CHUNKS
    fsdp_at = lax.axis_index("fsdp")
    x_at = (fsdp_at // 2).astype(jnp.int32)[None]
    z_at = (fsdp_at % 2).astype(jnp.int32)[None]

    start = local_weight[0]
    total = lax.dynamic_slice_in_dim(start, fragment[0] * piece_width, piece_width, 1)
    rep_bits = [1, 8, 16, 2, 4]

    def add_replicas(total):
        bit = rep_bits.pop(0)
        total = total.astype(jnp.float32) + rep_swap(total, bit).astype(jnp.float32)
        return total.astype(jnp.bfloat16) if rep_bits else total

    other = z_swap(start)
    cuts = [arrange(x_at, tokens, s) for s in range(steps)]
    masked = [
        jnp.where((token_ids[0, s] != pad_token)[:, None], out_grad[0, s], 0)
        for s in range(steps)
    ]

    def spread(pieces):
        return [pieces[0]] + [x_shift(pieces[o], o) for o in range(1, XS)]

    state = [(adam_first[0], adam_second[0], start, other, c) for c in range(CHUNKS)]
    total = add_replicas(total)
    blocks = spread(cuts[0])
    last = after(cuts[1][0], *masked)
    finished = ()
    for step in range(steps):
        parts, backs, grads = {}, {}, {}
        for c in range(CHUNKS):
            first, second, weight, other, column = state[c]
            parts[c] = forward(z_at, blocks, after(weight, last), other, column, chunk)
            last = parts[c][0]
        for c in range(CHUNKS):
            gathered = [parts[c][0]] + [x_shift(parts[c][o], -o) for o in range(1, XS)]
            gathered[0] = after(gathered[0], last)
            last = slope(proj_scale, gathered, masked[step], c)
            backs[c] = last
        for c in range(CHUNKS):
            spread_backs = [after(backs[c], last)] + [x_shift(backs[c], o) for o in range(1, XS)]
            grads[c] = backward(proj_scale, z_at, blocks, spread_backs)
            last = grads[c][0]
        if step + 1 < steps:
            blocks_next = spread([after(cut, *spread_backs) for cut in cuts[step + 1]])
        for c in range(CHUNKS):
            first, second, weight, other, column = state[c]
            mine, theirs = grads[c]
            received = z_swap(theirs)
            mine = after(mine, last)
            if step + 1 < steps:
                total = add_replicas(after(total, last))
                mine = after(mine, total)
                first, second, weight = adam(mine, received, first, second, weight, column)
                last = first
                total = add_replicas(after(total, last))
                last = after(last, total)
                state[c] = (first, second, weight, z_swap(weight), 0)
                if not rep_bits:
                    average = jnp.tile(total / lax.axis_size("rep"), (1, FRAGS))
                    rostered = (
                        lax.broadcasted_iota(jnp.int32, (1, columns), 1) // piece_width
                        == fragment[0]
                    )
                    pseudo = anchor - average
                    moment_new = outer_mu * outer_momentum + pseudo
                    anchor_new = anchor - outer_rate * (pseudo + outer_mu * moment_new)
                    new_anchor = jnp.where(rostered, anchor_new, anchor)
                    new_momentum = jnp.where(rostered, moment_new, outer_momentum)
            else:
                finished = finish(
                    fragment, mine, received, first, second, weight, new_anchor, finished, c
                )
                last = finished[0]
        if step + 1 < steps:
            blocks = blocks_next
    new_first, new_second, new_local = finished
    return (new_local[None], new_first[None], new_second[None], new_anchor, new_momentum)


def solution(mesh):
    return jax.shard_map(
        local,
        mesh=mesh,
        in_specs=(
            P("rep", None, "fsdp", None),
            P("rep", None, "fsdp"),
            P("rep", None, "fsdp", None),
            P("rep", "fsdp", None),
            P("rep", "fsdp", None),
            P("rep", "fsdp", None),
            P("fsdp", None),
            P("fsdp", None),
            P(),
        ),
        out_specs=(
            P("rep", "fsdp", None),
            P("rep", "fsdp", None),
            P("rep", "fsdp", None),
            P("fsdp", None),
            P("fsdp", None),
        ),
        check_vma=False,
    )
```

```python
import functools
import math

import jax
import jax.numpy as jnp
from jax import lax
from jax.experimental import pallas as pl
from jax.experimental.pallas import tpu as pltpu
from jax.sharding import PartitionSpec as P

FRAGS = 2
CHUNKS = 2

beta_first = 0.5
beta_second = 0.95
inner_rate = 0.25
decay_rate = 0.1
adam_eps = 1e-08
outer_rate = 0.7
outer_mu = 0.9
mix_keep = 0.5
pad_token = 128004
XS = 4
VMEM = 12 * 1024 * 1024


def z_swap(array):
    return lax.ppermute(array, "fsdp", [(i, i ^ 1) for i in range(2 * XS)])


def x_shift(array, offset):
    pairs = [
        (x * 2 + z, ((x + offset) % XS) * 2 + z) for x in range(XS) for z in range(2)
    ]
    return lax.ppermute(array, "fsdp", pairs)


def rep_swap(array, bit):
    return lax.ppermute(array, "rep", [(i, i ^ bit) for i in range(32)])


def after(value, *earlier):
    return lax.optimization_barrier((value, *earlier))[0]


def params():
    return pltpu.CompilerParams(vmem_limit_bytes=VMEM)


def cost():
    return pl.CostEstimate(flops=1000, bytes_accessed=1000, transcendentals=0)


def copy_body(x_at, *refs):
    for source, target in zip(refs[:XS], refs[XS:], strict=True):
        target[...] = source[0, 0]


def arrange(x_at, tokens, step):
    count, width = tokens.shape[2:]
    cut = width // XS
    tile = count // 2

    def taken(offset):
        return lambda i, x: (0, step, i, lax.rem(x[0] + offset, XS))

    return pl.pallas_call(
        copy_body,
        grid_spec=pltpu.PrefetchScalarGridSpec(
            num_scalar_prefetch=1,
            grid=(count // tile,),
            in_specs=[pl.BlockSpec((1, 1, tile, cut), taken(o)) for o in range(XS)],
            out_specs=[pl.BlockSpec((tile, cut), lambda i, x: (i, 0))] * XS,
        ),
        out_shape=[jax.ShapeDtypeStruct((count, cut), tokens.dtype)] * XS,
        compiler_params=params(),
        cost_estimate=cost(),
    )(x_at, *[tokens] * XS)


def halves_of(block, z_at):
    rows = block.shape[1] // 2
    mine = block[:, pl.ds(pl.multiple_of(z_at * rows, rows), rows)]
    theirs = block[:, pl.ds(pl.multiple_of((1 - z_at) * rows, rows), rows)]
    return mine, theirs


def forward_body(z_at, *refs):
    blocks, (weight, other), parts = refs[:XS], refs[XS : XS + 2], refs[XS + 2 :]
    for block, part in zip(blocks, parts, strict=True):
        mine, theirs = halves_of(block, z_at[0])
        total = jnp.dot(mine, weight[...], preferred_element_type=jnp.float32)
        total += jnp.dot(theirs, other[...], preferred_element_type=jnp.float32)
        part[...] = total.astype(part.dtype)


def forward(z_at, blocks, weight, other, column, chunk):
    count, cut = blocks[0].shape
    rows = cut // 2
    tile = count // 2
    weights = pl.BlockSpec((rows, chunk), lambda i, z: (0, column))
    return pl.pallas_call(
        forward_body,
        grid_spec=pltpu.PrefetchScalarGridSpec(
            num_scalar_prefetch=1,
            grid=(count // tile,),
            in_specs=[pl.BlockSpec((tile, cut), lambda i, z: (i, 0))] * XS + [weights] * 2,
            out_specs=[pl.BlockSpec((tile, chunk), lambda i, z: (i, 0))] * XS,
        ),
        out_shape=[
            jax.ShapeDtypeStruct((count, chunk), jnp.bfloat16 if o else jnp.float32)
            for o in range(XS)
        ],
        compiler_params=params(),
        cost_estimate=cost(),
    )(z_at, *blocks, weight, other)


def slope_body(scale, *refs):
    parts, grads, back = refs[:XS], refs[XS], refs[XS + 1]
    scores = parts[0][...]
    for part in parts[1:]:
        scores += part[...].astype(jnp.float32)
    scores = scale * scores
    logistic = jax.nn.sigmoid(scores)
    slope = logistic * (1.0 + scores * (1.0 - logistic))
    back[...] = (grads[...].astype(jnp.float32) * slope).astype(back.dtype)


def slope(scale, parts, grads, column):
    count, chunk = parts[0].shape
    tile = count // 2
    own = pl.BlockSpec((tile, chunk), lambda i: (i, 0))
    return pl.pallas_call(
        functools.partial(slope_body, scale),
        grid=(count // tile,),
        in_specs=[own] * XS + [pl.BlockSpec((tile, chunk), lambda i: (i, column))],
        out_specs=own,
        out_shape=jax.ShapeDtypeStruct((count, chunk), jnp.bfloat16),
        compiler_params=params(),
        cost_estimate=cost(),
    )(*parts, grads)


def backward_body(scale, z_at, *refs):
    blocks, backs = refs[:XS], refs[XS : 2 * XS]
    mine, theirs, mine_sum, theirs_sum = refs[2 * XS :]
    at = pl.program_id(0)

    @pl.when(at == 0)
    def _():
        mine_sum[...] = jnp.zeros_like(mine_sum)
        theirs_sum[...] = jnp.zeros_like(theirs_sum)

    for total, half in ((theirs_sum, 1), (mine_sum, 0)):
        more = 0.0
        for block, back in zip(blocks, backs, strict=True):
            more += lax.dot_general(
                halves_of(block, z_at[0])[half],
                back[...],
                (((0,), (0,)), ((), ())),
                preferred_element_type=jnp.float32,
            )
        total[...] += more

    @pl.when(at == pl.num_programs(0) - 1)
    def _():
        mine[...] = scale * mine_sum[...]
        theirs[...] = (scale * theirs_sum[...]).astype(theirs.dtype)


def backward(scale, z_at, blocks, backs):
    count, cut = blocks[0].shape
    chunk = backs[0].shape[1]
    rows = cut // 2
    tile = count // 2
    out = pl.BlockSpec((rows, chunk), lambda i, z: (0, 0))
    return pl.pallas_call(
        functools.partial(backward_body, scale),
        grid_spec=pltpu.PrefetchScalarGridSpec(
            num_scalar_prefetch=1,
            grid=(count // tile,),
            in_specs=[pl.BlockSpec((tile, cut), lambda i, z: (i, 0))] * XS
            + [pl.BlockSpec((tile, chunk), lambda i, z: (i, 0))] * XS,
            out_specs=[out, out],
            scratch_shapes=[pltpu.VMEM((rows, chunk), jnp.float32)] * 2,
        ),
        out_shape=[
            jax.ShapeDtypeStruct((rows, chunk), jnp.float32),
            jax.ShapeDtypeStruct((rows, chunk), jnp.bfloat16),
        ],
        compiler_params=params(),
        cost_estimate=cost(),
    )(z_at, *blocks, *backs)


def adam_values(mine, received, first, second, weight):
    grad = mine[...] + received[...].astype(jnp.float32)
    first = beta_first * first[...] + (1.0 - beta_first) * grad
    second = beta_second * second[...] + (1.0 - beta_second) * grad * grad
    master = weight[...].astype(jnp.float32)
    master = master - inner_rate * (
        first / (jnp.sqrt(second) + adam_eps) + decay_rate * master
    )
    return first, second, master.astype(jnp.bfloat16)


def adam_body(mine, received, first, second, weight, first_out, second_out, weight_out):
    first_out[...], second_out[...], weight_out[...] = adam_values(
        mine, received, first, second, weight
    )


def adam(mine, received, first, second, weight, column):
    rows, chunk = mine.shape
    height = rows // 2
    own = pl.BlockSpec((height, chunk), lambda i: (i, 0))
    whole = pl.BlockSpec((height, chunk), lambda i: (i, column))
    return pl.pallas_call(
        adam_body,
        grid=(rows // height,),
        in_specs=[own, own, whole, whole, whole],
        out_specs=[own, own, own],
        out_shape=[
            jax.ShapeDtypeStruct((rows, chunk), jnp.float32),
            jax.ShapeDtypeStruct((rows, chunk), jnp.float32),
            jax.ShapeDtypeStruct((rows, chunk), jnp.bfloat16),
        ],
        compiler_params=params(),
        cost_estimate=cost(),
    )(mine, received, first, second, weight)


def finish_body(
    column, fragment, mine, received, first, second, weight, anchor, *rest
):
    first_out, second_out, weight_out = rest[-3:]
    first_out[...], second_out[...], trained = adam_values(
        mine, received, first, second, weight
    )
    chunk = trained.shape[1]
    lanes = lax.broadcasted_iota(jnp.int32, trained.shape, 1) + column * chunk
    rostered = lanes // (CHUNKS * chunk // FRAGS) == fragment[0]
    mixed = mix_keep * trained.astype(jnp.float32) + (1.0 - mix_keep) * anchor[...]
    weight_out[...] = jnp.where(rostered, mixed.astype(jnp.bfloat16), trained)


def finish(fragment, mine, received, first, second, weight, anchor, earlier, column):
    rows, chunk = mine.shape
    height = rows // 2
    own = pl.BlockSpec((height, chunk), lambda i, f: (i, 0))
    whole = pl.BlockSpec((height, chunk), lambda i, f: (i, column))
    shape = (rows, chunk * CHUNKS)
    return pl.pallas_call(
        functools.partial(finish_body, column),
        grid_spec=pltpu.PrefetchScalarGridSpec(
            num_scalar_prefetch=1,
            grid=(rows // height,),
            in_specs=[own] * 5 + [whole] + [pl.BlockSpec(memory_space=pl.ANY)] * len(earlier),
            out_specs=[whole] * 3,
        ),
        out_shape=[
            jax.ShapeDtypeStruct(shape, jnp.float32),
            jax.ShapeDtypeStruct(shape, jnp.float32),
            jax.ShapeDtypeStruct(shape, jnp.bfloat16),
        ],
        input_output_aliases={7 + i: i for i in range(len(earlier))},
        compiler_params=params(),
        cost_estimate=cost(),
    )(fragment, mine, received, first, second, weight, anchor, *earlier)


def local(
    tokens,
    token_ids,
    out_grad,
    local_weight,
    adam_first,
    adam_second,
    anchor,
    outer_momentum,
    fragment,
):
    steps, token_count, width = tokens.shape[1:]
    proj_scale = 1.0 / math.sqrt(width)
    columns = local_weight.shape[2]
    piece_width = columns // FRAGS
    chunk = columns // CHUNKS
    fsdp_at = lax.axis_index("fsdp")
    x_at = (fsdp_at // 2).astype(jnp.int32)[None]
    z_at = (fsdp_at % 2).astype(jnp.int32)[None]

    start = local_weight[0]
    total = lax.dynamic_slice_in_dim(start, fragment[0] * piece_width, piece_width, 1)
    rep_bits = [1, 8, 16, 2, 4]

    def add_replicas(total):
        bit = rep_bits.pop(0)
        total = total.astype(jnp.float32) + rep_swap(total, bit).astype(jnp.float32)
        return total.astype(jnp.bfloat16) if rep_bits else total

    other = z_swap(start)
    cuts = [arrange(x_at, tokens, s) for s in range(steps)]
    masked = [
        jnp.where((token_ids[0, s] != pad_token)[:, None], out_grad[0, s], 0)
        for s in range(steps)
    ]

    def spread(pieces):
        return [pieces[0]] + [x_shift(pieces[o], o) for o in range(1, XS)]

    state = [(adam_first[0], adam_second[0], start, other, c) for c in range(CHUNKS)]
    for _ in range(5):
        total = add_replicas(total)
    average = jnp.tile(total / lax.axis_size("rep"), (1, FRAGS))
    rostered = lax.broadcasted_iota(jnp.int32, (1, columns), 1) // piece_width == fragment[0]
    pseudo = anchor - average
    moment_new = outer_mu * outer_momentum + pseudo
    anchor_new = anchor - outer_rate * (pseudo + outer_mu * moment_new)
    new_anchor = jnp.where(rostered, anchor_new, anchor)
    new_momentum = jnp.where(rostered, moment_new, outer_momentum)
    blocks = spread(cuts[0])
    last = after(cuts[1][0], *masked)
    finished = ()
    for step in range(steps):
        parts, backs, grads = {}, {}, {}
        for c in range(CHUNKS):
            first, second, weight, other, column = state[c]
            parts[c] = forward(z_at, blocks, after(weight, last), other, column, chunk)
            last = parts[c][0]
        for c in range(CHUNKS):
            gathered = [parts[c][0]] + [x_shift(parts[c][o], -o) for o in range(1, XS)]
            gathered[0] = after(gathered[0], last)
            last = slope(proj_scale, gathered, masked[step], c)
            backs[c] = last
        for c in range(CHUNKS):
            spread_backs = [after(backs[c], last)] + [x_shift(backs[c], o) for o in range(1, XS)]
            grads[c] = backward(proj_scale, z_at, blocks, spread_backs)
            last = grads[c][0]
        if step + 1 < steps:
            blocks_next = spread([after(cut, *spread_backs) for cut in cuts[step + 1]])
        for c in range(CHUNKS):
            first, second, weight, other, column = state[c]
            mine, theirs = grads[c]
            received = z_swap(theirs)
            mine = after(mine, last)
            if step + 1 < steps:
                first, second, weight = adam(mine, received, first, second, weight, column)
                last = first
                state[c] = (first, second, weight, z_swap(weight), 0)
            else:
                finished = finish(
                    fragment, mine, received, first, second, weight, new_anchor, finished, c
                )
                last = finished[0]
        if step + 1 < steps:
            blocks = blocks_next
    new_first, new_second, new_local = finished
    return (new_local[None], new_first[None], new_second[None], new_anchor, new_momentum)


def solution(mesh):
    return jax.shard_map(
        local,
        mesh=mesh,
        in_specs=(
            P("rep", None, "fsdp", None),
            P("rep", None, "fsdp"),
            P("rep", None, "fsdp", None),
            P("rep", "fsdp", None),
            P("rep", "fsdp", None),
            P("rep", "fsdp", None),
            P("fsdp", None),
            P("fsdp", None),
            P(),
        ),
        out_specs=(
            P("rep", "fsdp", None),
            P("rep", "fsdp", None),
            P("rep", "fsdp", None),
            P("fsdp", None),
            P("fsdp", None),
        ),
        check_vma=False,
    )
```

```python
import functools
import math

import jax
import jax.numpy as jnp
from jax import lax
from jax.experimental import pallas as pl
from jax.experimental.pallas import tpu as pltpu
from jax.sharding import PartitionSpec as P

FRAGS = 2
CHUNKS = 2

beta_first = 0.5
beta_second = 0.95
inner_rate = 0.25
decay_rate = 0.1
adam_eps = 1e-08
outer_rate = 0.7
outer_mu = 0.9
mix_keep = 0.5
pad_token = 128004
XS = 4
FIRST_VMEM = 60 * 1024 * 1024
VMEM = 12 * 1024 * 1024


def z_swap(array):
    return lax.ppermute(array, "fsdp", [(i, i ^ 1) for i in range(2 * XS)])


def x_shift(array, offset):
    pairs = [
        (x * 2 + z, ((x + offset) % XS) * 2 + z) for x in range(XS) for z in range(2)
    ]
    return lax.ppermute(array, "fsdp", pairs)


def rep_swap(array, bit):
    return lax.ppermute(array, "rep", [(i, i ^ bit) for i in range(32)])


def after(value, *earlier):
    return lax.optimization_barrier((value, *earlier))[0]


def params():
    return pltpu.CompilerParams(vmem_limit_bytes=VMEM)


def cost():
    return pl.CostEstimate(flops=1000, bytes_accessed=1000, transcendentals=0)


def copy_body(x_at, *refs):
    for source, target in zip(refs[:XS], refs[XS:], strict=True):
        target[...] = source[0, 0]


def arrange(x_at, tokens, step, limit):
    count, width = tokens.shape[2:]
    cut = width // XS
    tile = count // 2

    def taken(offset):
        return lambda i, x: (0, step, i, lax.rem(x[0] + offset, XS))

    return pl.pallas_call(
        copy_body,
        grid_spec=pltpu.PrefetchScalarGridSpec(
            num_scalar_prefetch=1,
            grid=(count // tile,),
            in_specs=[pl.BlockSpec((1, 1, tile, cut), taken(o)) for o in range(XS)],
            out_specs=[pl.BlockSpec((tile, cut), lambda i, x: (i, 0))] * XS,
        ),
        out_shape=[jax.ShapeDtypeStruct((count, cut), tokens.dtype)] * XS,
        compiler_params=pltpu.CompilerParams(vmem_limit_bytes=limit),
        cost_estimate=cost(),
    )(x_at, *[tokens] * XS)


def halves_of(block, z_at):
    rows = block.shape[1] // 2
    mine = block[:, pl.ds(pl.multiple_of(z_at * rows, rows), rows)]
    theirs = block[:, pl.ds(pl.multiple_of((1 - z_at) * rows, rows), rows)]
    return mine, theirs


def forward_body(z_at, *refs):
    blocks, (weight, other), parts = refs[:XS], refs[XS : XS + 2], refs[XS + 2 :]
    for block, part in zip(blocks, parts, strict=True):
        mine, theirs = halves_of(block, z_at[0])
        total = jnp.dot(mine, weight[...], preferred_element_type=jnp.float32)
        total += jnp.dot(theirs, other[...], preferred_element_type=jnp.float32)
        part[...] = total.astype(part.dtype)


def forward(z_at, blocks, weight, other, column, chunk):
    count, cut = blocks[0].shape
    rows = cut // 2
    tile = count // 2
    weights = pl.BlockSpec((rows, chunk), lambda i, z: (0, column))
    return pl.pallas_call(
        forward_body,
        grid_spec=pltpu.PrefetchScalarGridSpec(
            num_scalar_prefetch=1,
            grid=(count // tile,),
            in_specs=[pl.BlockSpec((tile, cut), lambda i, z: (i, 0))] * XS + [weights] * 2,
            out_specs=[pl.BlockSpec((tile, chunk), lambda i, z: (i, 0))] * XS,
        ),
        out_shape=[
            jax.ShapeDtypeStruct((count, chunk), jnp.bfloat16 if o else jnp.float32)
            for o in range(XS)
        ],
        compiler_params=params(),
        cost_estimate=cost(),
    )(z_at, *blocks, weight, other)


def slope_body(scale, *refs):
    parts, grads, back = refs[:XS], refs[XS], refs[XS + 1]
    scores = parts[0][...]
    for part in parts[1:]:
        scores += part[...].astype(jnp.float32)
    scores = scale * scores
    logistic = jax.nn.sigmoid(scores)
    slope = logistic * (1.0 + scores * (1.0 - logistic))
    back[...] = (grads[...].astype(jnp.float32) * slope).astype(back.dtype)


def slope(scale, parts, grads, column):
    count, chunk = parts[0].shape
    tile = count // 2
    own = pl.BlockSpec((tile, chunk), lambda i: (i, 0))
    return pl.pallas_call(
        functools.partial(slope_body, scale),
        grid=(count // tile,),
        in_specs=[own] * XS + [pl.BlockSpec((tile, chunk), lambda i: (i, column))],
        out_specs=own,
        out_shape=jax.ShapeDtypeStruct((count, chunk), jnp.bfloat16),
        compiler_params=params(),
        cost_estimate=cost(),
    )(*parts, grads)


def backward_body(scale, z_at, *refs):
    blocks, backs = refs[:XS], refs[XS : 2 * XS]
    mine, theirs, mine_sum, theirs_sum = refs[2 * XS :]
    at = pl.program_id(0)

    @pl.when(at == 0)
    def _():
        mine_sum[...] = jnp.zeros_like(mine_sum)
        theirs_sum[...] = jnp.zeros_like(theirs_sum)

    for total, half in ((theirs_sum, 1), (mine_sum, 0)):
        more = 0.0
        for block, back in zip(blocks, backs, strict=True):
            more += lax.dot_general(
                halves_of(block, z_at[0])[half],
                back[...],
                (((0,), (0,)), ((), ())),
                preferred_element_type=jnp.float32,
            )
        total[...] += more

    @pl.when(at == pl.num_programs(0) - 1)
    def _():
        mine[...] = scale * mine_sum[...]
        theirs[...] = (scale * theirs_sum[...]).astype(theirs.dtype)


def backward(scale, z_at, blocks, backs):
    count, cut = blocks[0].shape
    chunk = backs[0].shape[1]
    rows = cut // 2
    tile = count // 2
    out = pl.BlockSpec((rows, chunk), lambda i, z: (0, 0))
    return pl.pallas_call(
        functools.partial(backward_body, scale),
        grid_spec=pltpu.PrefetchScalarGridSpec(
            num_scalar_prefetch=1,
            grid=(count // tile,),
            in_specs=[pl.BlockSpec((tile, cut), lambda i, z: (i, 0))] * XS
            + [pl.BlockSpec((tile, chunk), lambda i, z: (i, 0))] * XS,
            out_specs=[out, out],
            scratch_shapes=[pltpu.VMEM((rows, chunk), jnp.float32)] * 2,
        ),
        out_shape=[
            jax.ShapeDtypeStruct((rows, chunk), jnp.float32),
            jax.ShapeDtypeStruct((rows, chunk), jnp.bfloat16),
        ],
        compiler_params=params(),
        cost_estimate=cost(),
    )(z_at, *blocks, *backs)


def adam_values(mine, received, first, second, weight):
    grad = mine[...] + received[...].astype(jnp.float32)
    first = beta_first * first[...] + (1.0 - beta_first) * grad
    second = beta_second * second[...] + (1.0 - beta_second) * grad * grad
    master = weight[...].astype(jnp.float32)
    master = master - inner_rate * (
        first / (jnp.sqrt(second) + adam_eps) + decay_rate * master
    )
    return first, second, master.astype(jnp.bfloat16)


def adam_body(mine, received, first, second, weight, first_out, second_out, weight_out):
    first_out[...], second_out[...], weight_out[...] = adam_values(
        mine, received, first, second, weight
    )


def adam(mine, received, first, second, weight, column):
    rows, chunk = mine.shape
    height = rows // 2
    own = pl.BlockSpec((height, chunk), lambda i: (i, 0))
    whole = pl.BlockSpec((height, chunk), lambda i: (i, column))
    return pl.pallas_call(
        adam_body,
        grid=(rows // height,),
        in_specs=[own, own, whole, whole, whole],
        out_specs=[own, own, own],
        out_shape=[
            jax.ShapeDtypeStruct((rows, chunk), jnp.float32),
            jax.ShapeDtypeStruct((rows, chunk), jnp.float32),
            jax.ShapeDtypeStruct((rows, chunk), jnp.bfloat16),
        ],
        compiler_params=params(),
        cost_estimate=cost(),
    )(mine, received, first, second, weight)


def finish_body(
    column, fragment, mine, received, first, second, weight, anchor, *rest
):
    first_out, second_out, weight_out = rest[-3:]
    first_out[...], second_out[...], trained = adam_values(
        mine, received, first, second, weight
    )
    chunk = trained.shape[1]
    lanes = lax.broadcasted_iota(jnp.int32, trained.shape, 1) + column * chunk
    rostered = lanes // (CHUNKS * chunk // FRAGS) == fragment[0]
    mixed = mix_keep * trained.astype(jnp.float32) + (1.0 - mix_keep) * anchor[...]
    weight_out[...] = jnp.where(rostered, mixed.astype(jnp.bfloat16), trained)


def finish(fragment, mine, received, first, second, weight, anchor, earlier, column):
    rows, chunk = mine.shape
    height = rows // 2
    own = pl.BlockSpec((height, chunk), lambda i, f: (i, 0))
    whole = pl.BlockSpec((height, chunk), lambda i, f: (i, column))
    shape = (rows, chunk * CHUNKS)
    return pl.pallas_call(
        functools.partial(finish_body, column),
        grid_spec=pltpu.PrefetchScalarGridSpec(
            num_scalar_prefetch=1,
            grid=(rows // height,),
            in_specs=[own] * 5 + [whole] + [pl.BlockSpec(memory_space=pl.ANY)] * len(earlier),
            out_specs=[whole] * 3,
        ),
        out_shape=[
            jax.ShapeDtypeStruct(shape, jnp.float32),
            jax.ShapeDtypeStruct(shape, jnp.float32),
            jax.ShapeDtypeStruct(shape, jnp.bfloat16),
        ],
        input_output_aliases={7 + i: i for i in range(len(earlier))},
        compiler_params=params(),
        cost_estimate=cost(),
    )(fragment, mine, received, first, second, weight, anchor, *earlier)


def local(
    tokens,
    token_ids,
    out_grad,
    local_weight,
    adam_first,
    adam_second,
    anchor,
    outer_momentum,
    fragment,
):
    steps, token_count, width = tokens.shape[1:]
    proj_scale = 1.0 / math.sqrt(width)
    columns = local_weight.shape[2]
    piece_width = columns // FRAGS
    chunk = columns // CHUNKS
    fsdp_at = lax.axis_index("fsdp")
    x_at = (fsdp_at // 2).astype(jnp.int32)[None]
    z_at = (fsdp_at % 2).astype(jnp.int32)[None]

    start = local_weight[0]
    total = lax.dynamic_slice_in_dim(start, fragment[0] * piece_width, piece_width, 1)
    rep_bits = [1, 2, 8, 16, 4]

    def add_replicas(total):
        bit = rep_bits.pop(0)
        total = total.astype(jnp.float32) + rep_swap(total, bit).astype(jnp.float32)
        return total.astype(jnp.bfloat16) if rep_bits else total

    other = z_swap(start)
    cuts = [arrange(x_at, tokens, s, VMEM if s else FIRST_VMEM) for s in range(steps)]
    masked = [
        jnp.where((token_ids[0, s] != pad_token)[:, None], out_grad[0, s], 0)
        for s in range(steps)
    ]

    def spread(pieces):
        return [pieces[0]] + [x_shift(pieces[o], o) for o in range(1, XS)]

    state = [(adam_first[0], adam_second[0], start, other, c) for c in range(CHUNKS)]
    for _ in range(len(rep_bits)):
        total = add_replicas(total)
    average = jnp.tile(total / lax.axis_size("rep"), (1, FRAGS))
    rostered = lax.broadcasted_iota(jnp.int32, (1, columns), 1) // piece_width == fragment[0]
    pseudo = anchor - average
    moment_new = outer_mu * outer_momentum + pseudo
    anchor_new = anchor - outer_rate * (pseudo + outer_mu * moment_new)
    new_anchor = jnp.where(rostered, anchor_new, anchor)
    new_momentum = jnp.where(rostered, moment_new, outer_momentum)
    blocks = spread(cuts[0])
    last = after(cuts[1][0], *masked)
    finished = ()
    for step in range(steps):
        parts, backs, grads = {}, {}, {}
        for c in range(CHUNKS):
            first, second, weight, other, column = state[c]
            parts[c] = forward(z_at, blocks, after(weight, last), other, column, chunk)
            last = parts[c][0]
        for c in range(CHUNKS):
            gathered = [parts[c][0]] + [x_shift(parts[c][o], -o) for o in range(1, XS)]
            gathered[0] = after(gathered[0], last)
            last = slope(proj_scale, gathered, masked[step], c)
            backs[c] = last
        for c in range(CHUNKS):
            spread_backs = [after(backs[c], last)] + [x_shift(backs[c], o) for o in range(1, XS)]
            grads[c] = backward(proj_scale, z_at, blocks, spread_backs)
            last = grads[c][0]
        if step + 1 < steps:
            blocks_next = spread([after(cut, *spread_backs) for cut in cuts[step + 1]])
        for c in range(CHUNKS):
            first, second, weight, other, column = state[c]
            mine, theirs = grads[c]
            received = z_swap(theirs)
            mine = after(mine, last)
            if step + 1 < steps:
                first, second, weight = adam(mine, received, first, second, weight, column)
                last = first
                state[c] = (first, second, weight, z_swap(weight), 0)
            else:
                finished = finish(
                    fragment, mine, received, first, second, weight, new_anchor, finished, c
                )
                last = finished[0]
        if step + 1 < steps:
            blocks = blocks_next
    new_first, new_second, new_local = finished
    return (new_local[None], new_first[None], new_second[None], new_anchor, new_momentum)


def solution(mesh):
    return jax.shard_map(
        local,
        mesh=mesh,
        in_specs=(
            P("rep", None, "fsdp", None),
            P("rep", None, "fsdp"),
            P("rep", None, "fsdp", None),
            P("rep", "fsdp", None),
            P("rep", "fsdp", None),
            P("rep", "fsdp", None),
            P("fsdp", None),
            P("fsdp", None),
            P(),
        ),
        out_specs=(
            P("rep", "fsdp", None),
            P("rep", "fsdp", None),
            P("rep", "fsdp", None),
            P("fsdp", None),
            P("fsdp", None),
        ),
        check_vma=False,
    )
```

```python
import functools
import math

import jax
import jax.numpy as jnp
from jax import lax
from jax.experimental import pallas as pl
from jax.experimental.pallas import tpu as pltpu
from jax.sharding import PartitionSpec as P

FRAGS = 2
CHUNKS = 2

beta_first = 0.5
beta_second = 0.95
inner_rate = 0.25
decay_rate = 0.1
adam_eps = 1e-08
outer_rate = 0.7
outer_mu = 0.9
mix_keep = 0.5
pad_token = 128004
XS = 4
FIRST_VMEM = 60 * 1024 * 1024
VMEM = 12 * 1024 * 1024


def z_swap(array):
    return lax.ppermute(array, "fsdp", [(i, i ^ 1) for i in range(2 * XS)])


def x_shift(array, offset):
    pairs = [
        (x * 2 + z, ((x + offset) % XS) * 2 + z) for x in range(XS) for z in range(2)
    ]
    return lax.ppermute(array, "fsdp", pairs)


def rep_swap(array, bit):
    return lax.ppermute(array, "rep", [(i, i ^ bit) for i in range(32)])


def after(value, *earlier):
    return lax.optimization_barrier((value, *earlier))[0]


def params():
    return pltpu.CompilerParams(vmem_limit_bytes=VMEM)


def cost():
    return pl.CostEstimate(flops=1000, bytes_accessed=1000, transcendentals=0)


def copy_body(x_at, *refs):
    for source, target in zip(refs[:XS], refs[XS:], strict=True):
        target[...] = source[0, 0]


def arrange(x_at, tokens, step, limit):
    count, width = tokens.shape[2:]
    cut = width // XS
    tile = count // 2

    def taken(offset):
        return lambda i, x: (0, step, i, lax.rem(x[0] + offset, XS))

    return pl.pallas_call(
        copy_body,
        grid_spec=pltpu.PrefetchScalarGridSpec(
            num_scalar_prefetch=1,
            grid=(count // tile,),
            in_specs=[pl.BlockSpec((1, 1, tile, cut), taken(o)) for o in range(XS)],
            out_specs=[pl.BlockSpec((tile, cut), lambda i, x: (i, 0))] * XS,
        ),
        out_shape=[jax.ShapeDtypeStruct((count, cut), tokens.dtype)] * XS,
        compiler_params=pltpu.CompilerParams(vmem_limit_bytes=limit),
        cost_estimate=cost(),
    )(x_at, *[tokens] * XS)


def halves_of(block, z_at):
    rows = block.shape[1] // 2
    mine = block[:, pl.ds(pl.multiple_of(z_at * rows, rows), rows)]
    theirs = block[:, pl.ds(pl.multiple_of((1 - z_at) * rows, rows), rows)]
    return mine, theirs


def forward_body(z_at, *refs):
    blocks, (weight, other), parts = refs[:XS], refs[XS : XS + 2], refs[XS + 2 :]
    for block, part in zip(blocks, parts, strict=True):
        mine, theirs = halves_of(block, z_at[0])
        total = jnp.dot(mine, weight[...], preferred_element_type=jnp.float32)
        total += jnp.dot(theirs, other[...], preferred_element_type=jnp.float32)
        part[...] = total.astype(part.dtype)


def forward(z_at, blocks, weight, other, column, chunk):
    count, cut = blocks[0].shape
    rows = cut // 2
    tile = count // 2
    weights = pl.BlockSpec((rows, chunk), lambda i, z: (0, column))
    return pl.pallas_call(
        forward_body,
        grid_spec=pltpu.PrefetchScalarGridSpec(
            num_scalar_prefetch=1,
            grid=(count // tile,),
            in_specs=[pl.BlockSpec((tile, cut), lambda i, z: (i, 0))] * XS + [weights] * 2,
            out_specs=[pl.BlockSpec((tile, chunk), lambda i, z: (i, 0))] * XS,
        ),
        out_shape=[
            jax.ShapeDtypeStruct((count, chunk), jnp.bfloat16 if o else jnp.float32)
            for o in range(XS)
        ],
        compiler_params=params(),
        cost_estimate=cost(),
    )(z_at, *blocks, weight, other)


def slope_body(scale, *refs):
    parts, grads, back = refs[:XS], refs[XS], refs[XS + 1]
    scores = parts[0][...]
    for part in parts[1:]:
        scores += part[...].astype(jnp.float32)
    scores = scale * scores
    logistic = jax.nn.sigmoid(scores)
    slope = logistic * (1.0 + scores * (1.0 - logistic))
    back[...] = (grads[...].astype(jnp.float32) * slope).astype(back.dtype)


def slope(scale, parts, grads, column):
    count, chunk = parts[0].shape
    tile = count // 2
    own = pl.BlockSpec((tile, chunk), lambda i: (i, 0))
    return pl.pallas_call(
        functools.partial(slope_body, scale),
        grid=(count // tile,),
        in_specs=[own] * XS + [pl.BlockSpec((tile, chunk), lambda i: (i, column))],
        out_specs=own,
        out_shape=jax.ShapeDtypeStruct((count, chunk), jnp.bfloat16),
        compiler_params=params(),
        cost_estimate=cost(),
    )(*parts, grads)


def backward_body(scale, z_at, *refs):
    blocks, backs = refs[:XS], refs[XS : 2 * XS]
    mine, theirs, mine_sum, theirs_sum = refs[2 * XS :]
    at = pl.program_id(0)

    @pl.when(at == 0)
    def _():
        mine_sum[...] = jnp.zeros_like(mine_sum)
        theirs_sum[...] = jnp.zeros_like(theirs_sum)

    for total, half in ((theirs_sum, 1), (mine_sum, 0)):
        more = 0.0
        for block, back in zip(blocks, backs, strict=True):
            more += lax.dot_general(
                halves_of(block, z_at[0])[half],
                back[...],
                (((0,), (0,)), ((), ())),
                preferred_element_type=jnp.float32,
            )
        total[...] += more

    @pl.when(at == pl.num_programs(0) - 1)
    def _():
        mine[...] = scale * mine_sum[...]
        theirs[...] = (scale * theirs_sum[...]).astype(theirs.dtype)


def backward(scale, z_at, blocks, backs):
    count, cut = blocks[0].shape
    chunk = backs[0].shape[1]
    rows = cut // 2
    tile = count // 2
    out = pl.BlockSpec((rows, chunk), lambda i, z: (0, 0))
    return pl.pallas_call(
        functools.partial(backward_body, scale),
        grid_spec=pltpu.PrefetchScalarGridSpec(
            num_scalar_prefetch=1,
            grid=(count // tile,),
            in_specs=[pl.BlockSpec((tile, cut), lambda i, z: (i, 0))] * XS
            + [pl.BlockSpec((tile, chunk), lambda i, z: (i, 0))] * XS,
            out_specs=[out, out],
            scratch_shapes=[pltpu.VMEM((rows, chunk), jnp.float32)] * 2,
        ),
        out_shape=[
            jax.ShapeDtypeStruct((rows, chunk), jnp.float32),
            jax.ShapeDtypeStruct((rows, chunk), jnp.bfloat16),
        ],
        compiler_params=params(),
        cost_estimate=cost(),
    )(z_at, *blocks, *backs)


def adam_values(mine, received, first, second, weight):
    grad = mine[...] + received[...].astype(jnp.float32)
    first = beta_first * first[...] + (1.0 - beta_first) * grad
    second = beta_second * second[...] + (1.0 - beta_second) * grad * grad
    master = weight[...].astype(jnp.float32)
    master = master - inner_rate * (
        first / (jnp.sqrt(second) + adam_eps) + decay_rate * master
    )
    return first, second, master.astype(jnp.bfloat16)


def adam_body(mine, received, first, second, weight, first_out, second_out, weight_out):
    first_out[...], second_out[...], weight_out[...] = adam_values(
        mine, received, first, second, weight
    )


def adam(mine, received, first, second, weight, column):
    rows, chunk = mine.shape
    height = rows // 2
    own = pl.BlockSpec((height, chunk), lambda i: (i, 0))
    whole = pl.BlockSpec((height, chunk), lambda i: (i, column))
    return pl.pallas_call(
        adam_body,
        grid=(rows // height,),
        in_specs=[own, own, whole, whole, whole],
        out_specs=[own, own, own],
        out_shape=[
            jax.ShapeDtypeStruct((rows, chunk), jnp.float32),
            jax.ShapeDtypeStruct((rows, chunk), jnp.float32),
            jax.ShapeDtypeStruct((rows, chunk), jnp.bfloat16),
        ],
        compiler_params=params(),
        cost_estimate=cost(),
    )(mine, received, first, second, weight)


def finish_body(
    column, fragment, mine, received, first, second, weight, anchor, *rest
):
    first_out, second_out, weight_out = rest[-3:]
    first_out[...], second_out[...], trained = adam_values(
        mine, received, first, second, weight
    )
    chunk = trained.shape[1]
    lanes = lax.broadcasted_iota(jnp.int32, trained.shape, 1) + column * chunk
    rostered = lanes // (CHUNKS * chunk // FRAGS) == fragment[0]
    mixed = mix_keep * trained.astype(jnp.float32) + (1.0 - mix_keep) * anchor[...]
    weight_out[...] = jnp.where(rostered, mixed.astype(jnp.bfloat16), trained)


def finish(fragment, mine, received, first, second, weight, anchor, earlier, column):
    rows, chunk = mine.shape
    height = rows // 2
    own = pl.BlockSpec((height, chunk), lambda i, f: (i, 0))
    whole = pl.BlockSpec((height, chunk), lambda i, f: (i, column))
    shape = (rows, chunk * CHUNKS)
    return pl.pallas_call(
        functools.partial(finish_body, column),
        grid_spec=pltpu.PrefetchScalarGridSpec(
            num_scalar_prefetch=1,
            grid=(rows // height,),
            in_specs=[own] * 5 + [whole] + [pl.BlockSpec(memory_space=pl.ANY)] * len(earlier),
            out_specs=[whole] * 3,
        ),
        out_shape=[
            jax.ShapeDtypeStruct(shape, jnp.float32),
            jax.ShapeDtypeStruct(shape, jnp.float32),
            jax.ShapeDtypeStruct(shape, jnp.bfloat16),
        ],
        input_output_aliases={7 + i: i for i in range(len(earlier))},
        compiler_params=params(),
        cost_estimate=cost(),
    )(fragment, mine, received, first, second, weight, anchor, *earlier)


def local(
    tokens,
    token_ids,
    out_grad,
    local_weight,
    adam_first,
    adam_second,
    anchor,
    outer_momentum,
    fragment,
):
    steps, token_count, width = tokens.shape[1:]
    proj_scale = 1.0 / math.sqrt(width)
    columns = local_weight.shape[2]
    piece_width = columns // FRAGS
    chunk = columns // CHUNKS
    fsdp_at = lax.axis_index("fsdp")
    x_at = (fsdp_at // 2).astype(jnp.int32)[None]
    z_at = (fsdp_at % 2).astype(jnp.int32)[None]

    start = local_weight[0]
    total = lax.dynamic_slice_in_dim(start, fragment[0] * piece_width, piece_width, 1)
    rep_bits = [1, 2, 8, 16, 4]

    def add_replicas(total):
        bit = rep_bits.pop(0)
        total = total.astype(jnp.float32) + rep_swap(total, bit).astype(jnp.float32)
        return total.astype(jnp.bfloat16) if rep_bits else total

    other = z_swap(start)
    cuts = [arrange(x_at, tokens, s, VMEM if s else FIRST_VMEM) for s in range(steps)]
    masked = [
        jnp.where((token_ids[0, s] != pad_token)[:, None], out_grad[0, s], 0)
        for s in range(steps)
    ]

    def spread(pieces):
        return [pieces[0]] + [x_shift(pieces[o], o) for o in range(1, XS)]

    state = [(adam_first[0], adam_second[0], start, other, c) for c in range(CHUNKS)]
    for _ in range(len(rep_bits)):
        total = add_replicas(total)
    average = jnp.tile(total / lax.axis_size("rep"), (1, FRAGS))
    rostered = lax.broadcasted_iota(jnp.int32, (1, columns), 1) // piece_width == fragment[0]
    pseudo = anchor - average
    moment_new = outer_mu * outer_momentum + pseudo
    anchor_new = anchor - outer_rate * (pseudo + outer_mu * moment_new)
    new_anchor = jnp.where(rostered, anchor_new, anchor)
    new_momentum = jnp.where(rostered, moment_new, outer_momentum)
    blocks = spread(cuts[0])
    last = after(cuts[1][0], *masked)
    finished = ()
    for step in range(steps):
        parts, backs, grads = {}, {}, {}
        for c in range(CHUNKS):
            first, second, weight, other, column = state[c]
            parts[c] = forward(z_at, blocks, after(weight, last), other, column, chunk)
            last = parts[c][0]
        for c in range(CHUNKS):
            gathered = [parts[c][0]] + [x_shift(parts[c][o], -o) for o in range(1, XS)]
            gathered[0] = after(gathered[0], last)
            last = slope(proj_scale, gathered, masked[step], c)
            backs[c] = last
        for c in range(CHUNKS):
            spread_backs = [after(backs[c], last)] + [x_shift(backs[c], o) for o in range(1, XS)]
            grads[c] = backward(proj_scale, z_at, blocks, spread_backs)
            last = grads[c][0]
        if step + 1 < steps:
            blocks_next = spread([after(cut, grads[0][1]) for cut in cuts[step + 1]])
        for c in range(CHUNKS):
            first, second, weight, other, column = state[c]
            mine, theirs = grads[c]
            received = z_swap(theirs)
            mine = after(mine, last)
            if step + 1 < steps:
                first, second, weight = adam(mine, received, first, second, weight, column)
                last = first
                state[c] = (first, second, weight, z_swap(weight), 0)
            else:
                finished = finish(
                    fragment, mine, received, first, second, weight, new_anchor, finished, c
                )
                last = finished[0]
        if step + 1 < steps:
            blocks = blocks_next
    new_first, new_second, new_local = finished
    return (new_local[None], new_first[None], new_second[None], new_anchor, new_momentum)


def solution(mesh):
    return jax.shard_map(
        local,
        mesh=mesh,
        in_specs=(
            P("rep", None, "fsdp", None),
            P("rep", None, "fsdp"),
            P("rep", None, "fsdp", None),
            P("rep", "fsdp", None),
            P("rep", "fsdp", None),
            P("rep", "fsdp", None),
            P("fsdp", None),
            P("fsdp", None),
            P(),
        ),
        out_specs=(
            P("rep", "fsdp", None),
            P("rep", "fsdp", None),
            P("rep", "fsdp", None),
            P("fsdp", None),
            P("fsdp", None),
        ),
        check_vma=False,
    )
```
